32 devices in a mesh: section: 8 (over z, core), expert: 4 (over y, x).
Axes of the slice: x: 2, y: 2, z: 4, core: 2. Of those that a mesh axis runs over, the one named last changes fastest.
Arguments:
- residual: float32 [8, 512, 2048], P('section', 'expert')
- norm_gain: float32 [8, 2048], P('section'), may hold values from 0.1 to 1.9
- w_gate: bfloat16 [8, 4, 2048, 768], P('section', 'expert'), may hold values from -0.125 to 0.125
- w_up: bfloat16 [8, 4, 2048, 768], P('section', 'expert'), may hold values from -0.125 to 0.125
- w_down: bfloat16 [8, 4, 768, 2048], P('section', 'expert'), may hold values from -0.21875 to 0.21875
- route_ids: int32 [3, 8, 512, 2], P(None, 'section', 'expert'), may hold values from 0 to 3, as said below
- route_slots: int32 [3, 8, 512, 2], P(None, 'section', 'expert'), may hold values from 0 to 127, as said below
- combine_weights: float32 [3, 8, 512, 2], P(None, 'section', 'expert'), may hold values from 0.2 to 1
Outputs:
- residual_out: float32 [8, 512, 2048], P('section', 'expert')
The draws below stay inside these ranges and needn't reach their ends.
Inputs may be any that keep to these rules, and one draw needn't show every extreme that they name: `route_ids`: each token names 2 different experts. Split the rows of one index of expert (128 tokens) into two halves of 64 tokens in order: in each half no expert is named more than 128 // 2 times, and at every step and section one expert is named exactly 128 // 2 times in every half of every index of expert. `route_slots`: the slot of (token t, choice k) is the number of earlier (token, choice) pairs, tokens in order then choices, in the same half of the same index of expert that name the same expert, plus 128 // 2 in the second half; so a slot of one source and expert is used at most once.
All inputs are finite; a program needn't handle non-finite values.
Results may differ from the reference program's by a relative error of at most 0.0033.
Values may be sent and summed in bfloat16 or wider, within the bound.
No kernel may reach another device: no remote copies, remote signals or barrier semaphores. Data moves between devices by JAX's collectives and lax.ppermute only.
A program may use at most 64 MiB of HBM per device.

```python
import math
import jax
import jax.numpy as jnp
from jax import lax

D = 2048
FF = 768
TOP = 2
STEPS = 3
TOK_DEV = 128
EXPERTS = 4
TOKENS_MB = 512
CAP = 128
N_SECTION = 8
N_EXPERT = 4


def routing_table(key):
    base_key = jax.random.fold_in(key, 7)
    half_rows = TOK_DEV // 2
    hot_count = 4 * half_rows // EXPERTS
    rest_total = 2 * half_rows - hot_count
    first_full = min(hot_count, rest_total)
    places = jnp.arange(2 * half_rows, dtype=jnp.int32)
    expert_iota = jnp.arange(EXPERTS, dtype=jnp.int32)
    other_places = jnp.arange(EXPERTS - 1, dtype=jnp.int32)

    def block_counts(move_key, forced):
        spread_total = rest_total - forced * first_full
        spread_count = EXPERTS - 1 - forced
        quotient = spread_total // spread_count
        remainder = spread_total % spread_count
        spread_index = other_places - forced
        valid = spread_index >= 0
        safe_index = jnp.where(valid, spread_index, 0)
        base = jnp.where(valid, quotient + (safe_index < remainder).astype(jnp.int32), first_full).astype(jnp.int32)
        is_lead = valid & (safe_index % 2 == 0) & (safe_index + 1 < spread_count)
        is_follow = valid & (safe_index % 2 == 1)
        base_next = jnp.concatenate([base[1:], jnp.zeros((1,), jnp.int32)])
        most_move = jnp.where(is_lead, jnp.minimum(hot_count - base, base_next), 0).astype(jnp.int32)
        moves = jax.random.randint(move_key, (EXPERTS - 1,), 0, most_move + 1).astype(jnp.int32)
        moves = jnp.where(is_lead, moves, 0)
        moves_prev = jnp.concatenate([jnp.zeros((1,), jnp.int32), moves[:-1]])
        others = base + moves - jnp.where(is_follow, moves_prev, 0)
        return jnp.concatenate([jnp.full((1,), hot_count, jnp.int32), others.astype(jnp.int32)])

    def one_block(block_key, forced, expert_order):
        token_key, label_key, move_key = jax.random.split(block_key, 3)
        counts = block_counts(move_key, forced)
        ends = jnp.cumsum(counts)
        labels = jnp.sum((ends[None, :] <= places[:, None]).astype(jnp.int32), axis=1).astype(jnp.int32)
        paired = jnp.stack([labels[:half_rows], labels[half_rows:]], axis=1)
        token_order = jax.random.permutation(token_key, half_rows)
        others = jax.random.permutation(label_key, EXPERTS - 1)
        mapping = jnp.concatenate([expert_order[:1], expert_order[1:][others]]).astype(jnp.int32)
        chosen = mapping[paired[token_order]]
        flat_choice = chosen.reshape(-1)
        onehot = (flat_choice[:, None] == expert_iota[None, :]).astype(jnp.int32)
        before = jnp.cumsum(onehot, axis=0) - onehot
        slot_rank = jnp.sum(before * onehot, axis=1).reshape(half_rows, 2)
        return (chosen, slot_rank)

    def one_group(group_index):
        expert_order = jax.random.permutation(jax.random.fold_in(base_key, group_index), EXPERTS).astype(jnp.int32)
        block_numbers = jnp.arange(N_EXPERT * 2, dtype=jnp.int32)
        group_key = jax.random.fold_in(base_key, 1000003 + group_index)
        flag_key = jax.random.fold_in(base_key, 2000003 + group_index)
        mask_key, pick_key = jax.random.split(flag_key)
        random_flags = jax.random.randint(mask_key, (N_EXPERT * 2,), 0, 2).astype(jnp.int32)
        picked_block = jax.random.randint(pick_key, (), 0, N_EXPERT * 2).astype(jnp.int32)
        forced = jnp.maximum(random_flags, (block_numbers == picked_block).astype(jnp.int32))
        block_keys = jax.vmap(lambda number: jax.random.fold_in(group_key, number))(block_numbers)
        chosen, slot_rank = jax.vmap(one_block, in_axes=(0, 0, None))(block_keys, forced, expert_order)
        offsets = (block_numbers % 2)[:, None, None] * hot_count
        slot_rank = slot_rank + offsets
        return (chosen.reshape(N_EXPERT * TOK_DEV, 2), slot_rank.reshape(N_EXPERT * TOK_DEV, 2))
    groups = jnp.arange(STEPS * N_SECTION, dtype=jnp.int32)
    chosen, slot_rank = jax.vmap(one_group)(groups)
    return (chosen.reshape(STEPS, N_SECTION, N_EXPERT * TOK_DEV, 2), slot_rank.reshape(STEPS, N_SECTION, N_EXPERT * TOK_DEV, 2))


def draw_route_ids(key, part):
    return routing_table(key)[0].astype(jnp.int32)


def draw_route_slots(key, part):
    return routing_table(key)[1].astype(jnp.int32)


def draw_residual(key, part):
    first_key, second_key, third_key = jax.random.split(key, 3)
    shape = (N_SECTION, N_EXPERT * TOK_DEV, D)
    half_range = 0.5 * math.log(10.0)
    row_scale = jnp.exp(jax.random.uniform(second_key, (N_SECTION, N_EXPERT * TOK_DEV, 1), jnp.float32, -half_range, half_range))
    column_scale = jnp.exp(jax.random.uniform(third_key, (1, 1, D), jnp.float32, -half_range, half_range))
    values = jax.random.normal(first_key, shape, jnp.float32)
    return (values * row_scale * column_scale).astype(jnp.float32)


def levels(stream_key, dims, shards, least, largest):
    gain = 1.0
    for position, parts in shards:
        draws = jax.random.uniform(jax.random.fold_in(jax.random.fold_in(stream_key, 6), position), (parts,), jnp.float32, least / len(shards), largest / len(shards))
        gain = gain * jnp.repeat(jnp.exp(draws), dims[position] // parts).reshape((-1,) + (1,) * (len(dims) - 1 - position))
    return gain


def normal_values(stream_key, dims, spread, limit, cuts=(), kind=jnp.bfloat16):
    array = jax.random.normal(stream_key, dims, jnp.float32) * spread
    if len(cuts) > 0:
        array = levels(stream_key, dims, cuts, -0.22, 0.18) * array
    return jnp.clip(array, min=-limit, max=limit).astype(kind)


def setup_inputs(seed: int = 0) -> dict:
    seeds = jax.random.split(jax.random.key(seed), 9)
    return {
        "residual": draw_residual(jax.random.fold_in(seeds[8], 71), 0),
        "norm_gain": jnp.clip(1.0 + 0.18 * jax.random.normal(seeds[1], (N_SECTION, D), jnp.float32), 0.1, 1.9),
        "w_gate": normal_values(seeds[2], (N_SECTION, EXPERTS, D, FF), D ** -0.5, 0.125, ((0, 8), (1, 4))),
        "w_up": normal_values(seeds[3], (N_SECTION, EXPERTS, D, FF), D ** -0.5, 0.125, ((0, 8), (1, 4))),
        "w_down": normal_values(seeds[4], (N_SECTION, EXPERTS, FF, D), FF ** -0.5, 0.21875, ((0, 8), (1, 4))),
        "route_ids": draw_route_ids(jax.random.fold_in(seeds[8], 71), 0),
        "route_slots": draw_route_slots(jax.random.fold_in(seeds[8], 71), 0),
        "combine_weights": jnp.clip(0.2 + 0.8 * jax.random.uniform(seeds[7], (STEPS, N_SECTION, TOKENS_MB, TOP), jnp.float32) ** levels(seeds[7], (STEPS, N_SECTION, TOKENS_MB, TOP), ((1, 8), (2, 4)), -0.2, 0.2), 0.2, 1.0),
    }


def expert_ffn(rows_in, gate_mat, up_mat, down_mat):
    gate_part = jnp.dot(rows_in, gate_mat, preferred_element_type=jnp.float32)
    upward = jnp.dot(rows_in, up_mat, preferred_element_type=jnp.float32)
    hidden = (jax.nn.silu(gate_part) * upward).astype(jnp.bfloat16)
    return jnp.dot(hidden, down_mat, preferred_element_type=jnp.float32).astype(jnp.bfloat16)

def rms_normed(current, gain_row):
    inv_rms = lax.rsqrt(lax.optimization_barrier(jnp.mean(current * current, axis=-1, keepdims=True)) + 1e-06)
    return (current * inv_rms * gain_row).astype(jnp.bfloat16)

def apply_layer(operands):
    current, gain_row, gate_all, up_all, down_all, chosen, slot_rows, weights_in = operands
    normed = rms_normed(current, gain_row)
    source = jnp.broadcast_to((jnp.arange(TOKENS_MB, dtype=jnp.int32) // TOK_DEV)[:, None], (TOKENS_MB, TOP))
    buffer = jnp.zeros((EXPERTS, N_EXPERT, CAP, D), jnp.bfloat16)
    buffer = buffer.at[chosen, source, slot_rows].set(jnp.broadcast_to(normed[:, None, :], (TOKENS_MB, TOP, D)))

    def per_expert(items):
        rows_in, gate_mat, up_mat, down_mat = items
        result = expert_ffn(rows_in.reshape(N_EXPERT * CAP, D), gate_mat, up_mat, down_mat)
        return result.reshape(N_EXPERT, CAP, D)
    outputs = lax.map(per_expert, (buffer, gate_all, up_all, down_all))
    picked = outputs[chosen, source, slot_rows]
    combined = lax.optimization_barrier(jnp.sum(weights_in[:, :, None] * picked.astype(jnp.float32), axis=1))
    return current + combined

def reference(residual, norm_gain, w_gate, w_up, w_down, route_ids, route_slots, combine_weights):
    current = residual
    for step_index in range(STEPS):
        current = lax.map(apply_layer, (current, norm_gain, w_gate, w_up, w_down, route_ids[step_index], route_slots[step_index], combine_weights[step_index]))
        current = jnp.roll(current, 1, axis=0)
    return current
```

```python
import jax
import jax.numpy as jnp
from jax import lax
from jax.experimental import pallas as pl
from jax.experimental.pallas import tpu as pltpu
from jax.sharding import PartitionSpec as P

TOP = 2
STEPS = 3
CHUNKS = 2
SHIFT = 2
LIMIT = 20 * 1024 * 1024


def shifted(x, axis, by):
    count = lax.axis_size(axis)
    return lax.ppermute(x, axis, [(i, (i + by) % count) for i in range(count)])


def rms_normed(current, gain_row):
    inv_rms = lax.rsqrt(jnp.mean(current * current, axis=-1, keepdims=True) + 1e-06)
    return (current * inv_rms * gain_row).astype(jnp.bfloat16)


def expert_ffn(rows_in, gate_mat, up_mat, down_mat):
    gate_part = jnp.dot(rows_in, gate_mat, preferred_element_type=jnp.float32)
    upward = jnp.dot(rows_in, up_mat, preferred_element_type=jnp.float32)
    hidden = (jax.nn.silu(gate_part) * upward).astype(jnp.bfloat16)
    return jnp.dot(hidden, down_mat, preferred_element_type=jnp.float32).astype(jnp.bfloat16)


def layer_by_slots(token_rows, gain_row, chosen, slot_rows, weights_in, experts, cap, mats):
    normed = rms_normed(token_rows, gain_row)
    flat_place = chosen * cap + slot_rows
    place_iota = jnp.arange(experts * cap, dtype=jnp.int32)
    tables = [
        (flat_place[:, k : k + 1] == place_iota[None, :]).astype(jnp.bfloat16) for k in range(TOP)
    ]
    occupied = tables[0] + tables[1]
    send = lax.dot_general(
        occupied, normed, (((0,), (0,)), ((), ())), preferred_element_type=jnp.float32
    )
    send = send.astype(jnp.bfloat16).reshape(experts, cap, normed.shape[1])
    received = lax.all_to_all(send, "expert", split_axis=0, concat_axis=0, tiled=True)
    result = expert_ffn(received.reshape(experts * cap, normed.shape[1]), *mats)
    returned = lax.all_to_all(
        result.reshape(send.shape), "expert", split_axis=0, concat_axis=0, tiled=True
    ).reshape(experts * cap, normed.shape[1])
    combined = jnp.zeros(token_rows.shape, jnp.float32)
    for k in range(TOP):
        picked = jnp.dot(tables[k], returned, preferred_element_type=jnp.float32)
        combined = combined + weights_in[:, k : k + 1] * picked
    return token_rows + combined


def run_by_slots(residual, norm_gain, mats, route_ids, route_slots, combine_weights):
    experts = lax.axis_size("expert")
    cap = 4 * residual.shape[1] // experts
    current = residual[0]
    for step in range(STEPS):
        current = layer_by_slots(
            current,
            norm_gain[0],
            route_ids[step, 0],
            route_slots[step, 0],
            combine_weights[step, 0],
            experts,
            cap,
            mats,
        )
        current = shifted(current, "section", 1)
    return current[None]


def across(x, bits):
    return lax.ppermute(x, "expert", [(e, e ^ bits) for e in range(4)])


def onward(x, bits):
    sections = lax.axis_size("section")
    pairs = [
        (s * 4 + e, ((s + 1) % sections) * 4 + (e ^ bits)) for s in range(sections) for e in range(4)
    ]
    return lax.ppermute(x, ("section", "expert"), pairs)


def norm_kernel(x_ref, gain_ref, normed_ref):
    x = x_ref[...]
    inv_rms = lax.rsqrt(jnp.mean(x * x, axis=-1, keepdims=True) + 1e-06)
    normed_ref[...] = (x * inv_rms * gain_ref[...]).astype(jnp.bfloat16)


def norm_rows(x, gain):
    return pl.pallas_call(
        norm_kernel,
        out_shape=jax.ShapeDtypeStruct(x.shape, jnp.bfloat16),
        compiler_params=pltpu.CompilerParams(vmem_limit_bytes=LIMIT),
        cost_estimate=pl.CostEstimate(flops=5 * x.size, bytes_accessed=6 * x.size, transcendentals=0),
    )(x, gain)


def total_kernel(x_ref, own_ref, a_ref, b_ref, gain_ref, new_ref, normed_ref):
    f32 = jnp.float32
    x = x_ref[...] + (own_ref[...].astype(f32) + a_ref[...].astype(f32) + b_ref[...].astype(f32))
    new_ref[...] = x
    inv_rms = lax.rsqrt(jnp.mean(x * x, axis=-1, keepdims=True) + 1e-06)
    normed_ref[...] = (x * inv_rms * gain_ref[...]).astype(jnp.bfloat16)


def total_rows(x, own, a, b, gain):
    return pl.pallas_call(
        total_kernel,
        out_shape=(
            jax.ShapeDtypeStruct(x.shape, jnp.float32),
            jax.ShapeDtypeStruct(x.shape, jnp.bfloat16),
        ),
        compiler_params=pltpu.CompilerParams(vmem_limit_bytes=LIMIT),
        cost_estimate=pl.CostEstimate(flops=8 * x.size, bytes_accessed=16 * x.size, transcendentals=0),
    )(x, own, a, b, gain)


def ffn_kernel(own, rx, ry, rd, weight, gate, up, down, o_own, o_x, o_y, o_d):
    f32 = jnp.float32
    n = own.shape[0]
    rows = jnp.concatenate([own[...], rx[...], ry[...], rd[...]], axis=0)
    gate_part = jnp.dot(rows, gate[...], preferred_element_type=f32)
    upward = jnp.dot(rows, up[...], preferred_element_type=f32)
    silu = gate_part / (1.0 + jnp.exp(-gate_part))
    hidden = (silu * upward * weight[...]).astype(jnp.bfloat16)
    out = jnp.dot(hidden, down[...], preferred_element_type=f32).astype(jnp.bfloat16)
    for j, ref in enumerate((o_own, o_x, o_y, o_d)):
        ref[...] = out[j * n : (j + 1) * n]


def weighted_ffn(pieces, weight, gate_mat, up_mat, down_mat):
    n, width = pieces[0].shape
    macs = 4 * n * gate_mat.size * 3
    return pl.pallas_call(
        ffn_kernel,
        out_shape=[jax.ShapeDtypeStruct((n, width), jnp.bfloat16)] * 4,
        compiler_params=pltpu.CompilerParams(vmem_limit_bytes=LIMIT),
        cost_estimate=pl.CostEstimate(
            flops=2 * macs, bytes_accessed=16 * n * width, transcendentals=4 * n * gate_mat.shape[1]
        ),
    )(*pieces, weight, gate_mat, up_mat, down_mat)


def run_by_rows(residual, norm_gain, mats, route_ids, combine_weights):
    me = lax.axis_index("expert")
    rows = residual.shape[1] // CHUNKS
    row_weights = []
    for bits in range(4):
        named = route_ids[:, 0] == (me ^ bits)
        weight = jnp.sum(jnp.where(named, combine_weights[:, 0], 0.0), axis=-1)
        row_weights.append(across(weight, bits) if bits else weight)
    row_weights = jnp.stack(row_weights, axis=1)
    gain = norm_gain
    next_gain = lax.ppermute(norm_gain, "section", [((i + 1) % 8, i) for i in range(8)]) if SHIFT == 2 else gain
    xs = [residual[0, c * rows : (c + 1) * rows] for c in range(CHUNKS)]
    firsts = []
    for c in range(CHUNKS):
        own = norm_rows(xs[c], gain)
        firsts.append((own, across(own, 1), across(own, 2)))
    for step in range(STEPS):
        for c in range(CHUNKS):
            one, two = (1, 2) if c % 2 == 0 else (2, 1)
            own, rx, ry = firsts[c]
            rd = across(rx, 2) if c % 2 == 0 else across(ry, 1)
            weight = row_weights[step, :, c * rows : (c + 1) * rows].reshape(4 * rows, 1)
            o_own, o_x, o_y, o_d = weighted_ffn((own, rx, ry, rd), weight, *mats)
            if c % 2 == 0:
                got_x = across(o_x, 1)
                got_y = across(o_y + across(o_d, 1), 2)
            else:
                got_y = across(o_y, 2)
                got_x = across(o_x + across(o_d, 2), 1)
            new, normed = total_rows(xs[c], o_own, got_x, got_y, next_gain)
            if step < STEPS - 1:
                if SHIFT == 2:
                    firsts[c] = (onward(normed, 0), onward(normed, 1), onward(normed, 2))
                    xs[c] = onward(new, 0)
                else:
                    xs[c] = onward(new, 0)
                    own = norm_rows(xs[c], gain)
                    firsts[c] = (own, across(own, 1), across(own, 2))
            else:
                xs[c] = onward(new, 0)
    return jnp.concatenate(xs, axis=0)[None]


def per_device(residual, norm_gain, w_gate, w_up, w_down, route_ids, route_slots, combine_weights):
    mats = (w_gate[0, 0], w_up[0, 0], w_down[0, 0])
    if lax.axis_size("expert") == 4:
        return run_by_rows(residual, norm_gain, mats, route_ids, combine_weights)
    return run_by_slots(residual, norm_gain, mats, route_ids, route_slots, combine_weights)


def solution(mesh):
    in_specs = (
        P("section", "expert", None),
        P("section", None),
        P("section", "expert", None, None),
        P("section", "expert", None, None),
        P("section", "expert", None, None),
        P(None, "section", "expert", None),
        P(None, "section", "expert", None),
        P(None, "section", "expert", None),
    )
    out_specs = P("section", "expert", None)
    return jax.shard_map(
        per_device, mesh=mesh, in_specs=in_specs, out_specs=out_specs, check_vma=False
    )
```

```python
import functools

import jax
import jax.numpy as jnp
from jax import lax
from jax.experimental import pallas as pl
from jax.experimental.pallas import tpu as pltpu
from jax.sharding import PartitionSpec as P

TOP = 2
STEPS = 3
SIZES = (64, 64)
MODE = ("rows", "rows")
LAST = ("whole", "whole")
CARRY = (False, False)
LIMIT = 16 * 1024 * 1024


def order(k):
    for step in range(STEPS):
        for what in range(4):
            for c in range(k):
                yield what, step + what // 3, c


def shifted(x, axis, by):
    count = lax.axis_size(axis)
    return lax.ppermute(x, axis, [(i, (i + by) % count) for i in range(count)])


def rms_normed(current, gain_row):
    inv_rms = lax.rsqrt(jnp.mean(current * current, axis=-1, keepdims=True) + 1e-06)
    return (current * inv_rms * gain_row).astype(jnp.bfloat16)


def expert_ffn(rows_in, gate_mat, up_mat, down_mat):
    gate_part = jnp.dot(rows_in, gate_mat, preferred_element_type=jnp.float32)
    upward = jnp.dot(rows_in, up_mat, preferred_element_type=jnp.float32)
    hidden = (jax.nn.silu(gate_part) * upward).astype(jnp.bfloat16)
    return jnp.dot(hidden, down_mat, preferred_element_type=jnp.float32).astype(jnp.bfloat16)


def layer_by_slots(token_rows, gain_row, chosen, slot_rows, weights_in, experts, cap, mats):
    normed = rms_normed(token_rows, gain_row)
    flat_place = chosen * cap + slot_rows
    place_iota = jnp.arange(experts * cap, dtype=jnp.int32)
    tables = [
        (flat_place[:, k : k + 1] == place_iota[None, :]).astype(jnp.bfloat16) for k in range(TOP)
    ]
    occupied = tables[0] + tables[1]
    send = lax.dot_general(
        occupied, normed, (((0,), (0,)), ((), ())), preferred_element_type=jnp.float32
    )
    send = send.astype(jnp.bfloat16).reshape(experts, cap, normed.shape[1])
    received = lax.all_to_all(send, "expert", split_axis=0, concat_axis=0, tiled=True)
    result = expert_ffn(received.reshape(experts * cap, normed.shape[1]), *mats)
    returned = lax.all_to_all(
        result.reshape(send.shape), "expert", split_axis=0, concat_axis=0, tiled=True
    ).reshape(experts * cap, normed.shape[1])
    combined = jnp.zeros(token_rows.shape, jnp.float32)
    for k in range(TOP):
        picked = jnp.dot(tables[k], returned, preferred_element_type=jnp.float32)
        combined = combined + weights_in[:, k : k + 1] * picked
    return token_rows + combined


def run_by_slots(residual, norm_gain, mats, route_ids, route_slots, combine_weights):
    experts = lax.axis_size("expert")
    cap = 4 * residual.shape[1] // experts
    current = residual[0]
    for step in range(STEPS):
        current = layer_by_slots(
            current,
            norm_gain[0],
            route_ids[step, 0],
            route_slots[step, 0],
            combine_weights[step, 0],
            experts,
            cap,
            mats,
        )
        current = shifted(current, "section", 1)
    return current[None]


def across(x, bits):
    return lax.ppermute(x, "expert", [(e, e ^ bits) for e in range(4)])


def onward(x, bits, by=1):
    sections = lax.axis_size("section")
    pairs = [
        (s * 4 + e, ((s + by) % sections) * 4 + (e ^ bits)) for s in range(sections) for e in range(4)
    ]
    return lax.ppermute(x, ("section", "expert"), pairs)


def normed_of(x, gain):
    inv_rms = lax.rsqrt(jnp.mean(x * x, axis=-1, keepdims=True) + 1e-06)
    return (x * inv_rms * gain).astype(jnp.bfloat16)


VMEM_SPEC = pl.BlockSpec(memory_space=pltpu.VMEM)
SMEM_SPEC = pl.BlockSpec(memory_space=pltpu.SMEM)
ANY_SPEC = pl.BlockSpec(memory_space=pl.ANY)
MARK = jax.ShapeDtypeStruct((8, 128), jnp.float32)


def call(kernel, outs, ins, specs, flops, moved, exps=0, scratch=()):
    return pl.pallas_call(
        kernel,
        in_specs=specs,
        out_shape=outs,
        scratch_shapes=scratch,
        compiler_params=pltpu.CompilerParams(vmem_limit_bytes=LIMIT),
        cost_estimate=pl.CostEstimate(flops=flops, bytes_accessed=moved, transcendentals=exps),
    )(*ins)


def far(x):
    return pltpu.with_memory_space_constraint(x, pltpu.HBM)


def bf16_rows(n, width):
    return jax.ShapeDtypeStruct((n, width), jnp.bfloat16)


def f32_rows(n, width):
    return jax.ShapeDtypeStruct((n, width), jnp.float32)


def start_kernel(me_ref, x_far, gain_far, ids_far, combine_far, *refs):
    x_refs, refs = refs[: len(SIZES)], refs[len(SIZES) :]
    normed_refs, refs = refs[: len(SIZES)], refs[len(SIZES) :]
    weight_refs, (mark, gain, ids, combine, sems) = refs[:4], refs[4:]
    copies = []
    at = 0
    for c, n in enumerate(SIZES):
        rows = x_far.at[0, pl.ds(at, n)]
        copies.append(pltpu.make_async_copy(rows, x_refs[c], sems.at[c]))
        at += n
    others = ((gain_far, gain), (ids_far, ids), (combine_far, combine))
    for j, (src, dst) in enumerate(others):
        copies.append(pltpu.make_async_copy(src, dst, sems.at[len(SIZES) + j]))
    for copy in copies:
        copy.start()
    mark[...] = jnp.zeros_like(mark)
    for copy in copies:
        copy.wait()
    for c in range(len(SIZES)):
        normed_refs[c][...] = normed_of(x_refs[c][...], gain[...])
    me = me_ref[0]
    for bits, out in enumerate(weight_refs):
        for step in range(STEPS):
            named = ids[step] == (me ^ bits)
            out[step : step + 1] = jnp.sum(
                jnp.where(named, combine[step], 0.0), axis=0, keepdims=True
            )


def start_rows(me, x, gain, ids, combine):
    width = x.shape[-1]
    outs = [f32_rows(n, width) for n in SIZES] + [bf16_rows(n, width) for n in SIZES]
    outs += [jax.ShapeDtypeStruct((STEPS, ids.shape[-1]), jnp.float32)] * 4 + [MARK]
    scratch = [
        pltpu.VMEM(gain.shape, jnp.float32),
        pltpu.VMEM(ids.shape, jnp.int32),
        pltpu.VMEM(combine.shape, jnp.float32),
        pltpu.SemaphoreType.DMA((len(SIZES) + 3,)),
    ]
    ins = (me, *(far(v) for v in (x, gain, ids, combine)))
    specs = [SMEM_SPEC] + [ANY_SPEC] * 4
    return call(start_kernel, outs, ins, specs, 5 * x.size, 6 * x.size, scratch=scratch)


def load_kernel(*refs):
    sems = refs[-1]
    mats, outs = refs[:3], refs[-4:-1]
    copies = [pltpu.make_async_copy(m, o, sems.at[j]) for j, (m, o) in enumerate(zip(mats, outs))]
    for copy in copies:
        copy.start()
    for copy in copies:
        copy.wait()


def load_mats(mats, before):
    outs = [pltpu.VMEM(m.shape, m.dtype) for m in mats]
    ins = (*(far(m) for m in mats), *before)
    size = sum(2 * m.size for m in mats)
    scratch = [pltpu.SemaphoreType.DMA((3,))]
    return call(load_kernel, outs, ins, [ANY_SPEC] * len(ins), 0, 2 * size, scratch=scratch)


def add_kernel(a_ref, b_ref, before, out_ref, mark):
    del before
    f32 = jnp.float32
    out_ref[...] = (a_ref[...].astype(f32) + b_ref[...].astype(f32)).astype(jnp.bfloat16)
    mark[...] = jnp.zeros_like(mark)


def add_rows(a, b, before):
    specs = [VMEM_SPEC] * 2 + [ANY_SPEC]
    outs = (bf16_rows(*a.shape), MARK)
    return call(add_kernel, outs, (a, b, before), specs, a.size, 6 * a.size)


def summed(x_ref, own_ref, a_ref, b_ref):
    f32 = jnp.float32
    return x_ref[...] + (own_ref[...].astype(f32) + a_ref[...].astype(f32) + b_ref[...].astype(f32))


def total_kernel(x_ref, own_ref, a_ref, b_ref, gain_ref, before, new_ref, normed_ref, mark):
    del before
    x = summed(x_ref, own_ref, a_ref, b_ref)
    new_ref[...] = x
    normed_ref[...] = normed_of(x, gain_ref[...])
    mark[...] = jnp.zeros_like(mark)


def total_rows(x, sums, gain, before):
    n, width = x.shape
    outs = [f32_rows(n, width), bf16_rows(n, width), MARK]
    specs = [VMEM_SPEC] * 5 + [ANY_SPEC]
    return call(total_kernel, outs, (x, *sums, gain, before), specs, 8 * n * width, 16 * n * width)


def add_total_kernel(x_ref, own_ref, a_ref, b_ref, before, new_ref, mark):
    del before
    new_ref[...] = summed(x_ref, own_ref, a_ref, b_ref)
    mark[...] = jnp.zeros_like(mark)


def add_total(x, sums, before):
    outs = [f32_rows(*x.shape), MARK]
    specs = [VMEM_SPEC] * 4 + [ANY_SPEC]
    return call(add_total_kernel, outs, (x, *sums, before), specs, 3 * x.size, 16 * x.size)


def renorm_kernel(x_ref, gain_ref, before, normed_ref, mark):
    del before
    normed_ref[...] = normed_of(x_ref[...], gain_ref[...])
    mark[...] = jnp.zeros_like(mark)


def renorm(x, gain, before):
    outs = [bf16_rows(*x.shape), MARK]
    return call(renorm_kernel, outs, (x, gain, before), [VMEM_SPEC] * 2 + [ANY_SPEC], 5 * x.size, 6 * x.size)


def final_kernel(counts, *refs):
    out = refs[-1]
    at = i = 0
    for n, count in zip(SIZES, counts):
        out[0, at : at + n] = refs[i][...] if count == 1 else summed(*refs[i : i + 4])
        at += n
        i += count


def final_rows(groups, shape):
    out = jax.ShapeDtypeStruct(shape, jnp.float32)
    size = shape[1] * shape[2]
    ins = [v for group in groups for v in group]
    kernel = functools.partial(final_kernel, tuple(len(group) for group in groups))
    return call(kernel, out, ins, [VMEM_SPEC] * len(ins), 3 * size, 14 * size)


def ffn_kernel(step, first, keep, own, rx, ry, rd, w0, w1, w2, w3, gate, up, down, before, *rest):
    del before
    f32 = jnp.float32
    n = own.shape[0]
    token = lax.broadcasted_iota(jnp.int32, (n, w0.shape[1]), 1)
    here = token == first + lax.broadcasted_iota(jnp.int32, (n, w0.shape[1]), 0)
    weight = [
        jnp.sum(jnp.where(here, w[step : step + 1], 0.0), axis=1, keepdims=True)
        for w in (w0, w1, w2, w3)
    ]
    weight = jnp.concatenate(weight, axis=0)
    rows = jnp.concatenate([own[...], rx[...], ry[...], rd[...]], axis=0)
    gate_part = jnp.dot(rows, gate[...], preferred_element_type=f32)
    upward = jnp.dot(rows, up[...], preferred_element_type=f32)
    silu = gate_part / (1.0 + jnp.exp(-gate_part))
    hidden = (silu * upward * weight).astype(jnp.bfloat16)
    out = jnp.dot(hidden, down[...], preferred_element_type=f32).astype(jnp.bfloat16)
    outs = rest[1:] if keep else rest
    for j in range(4):
        outs[j][...] = out[j * n : (j + 1) * n]
    outs[4][...] = jnp.zeros_like(outs[4])
    if keep:
        outs[5][...] = rest[0][...]


def weighted_ffn(step, first, pieces, weights, mats, before, carried=None):
    n, width = pieces[0].shape
    wide = mats[0].shape[1]
    macs = 4 * n * mats[0].size * 3
    keep = carried is not None
    kernel = functools.partial(ffn_kernel, step, first, keep)
    outs = [bf16_rows(n, width)] * 4 + [MARK]
    ins = (*pieces, *weights, *mats, before)
    specs = [VMEM_SPEC] * 11 + [ANY_SPEC]
    if keep:
        outs.append(f32_rows(n, width))
        ins += (carried,)
        specs.append(VMEM_SPEC)
    return call(kernel, outs, ins, specs, 2 * macs, 16 * n * width, 4 * n * wide)


def run_by_rows(residual, norm_gain, mats, route_ids, combine_weights):
    me = lax.axis_index("expert").reshape(1)
    sections = lax.axis_size("section")
    chunks = range(len(SIZES))
    starts = [sum(SIZES[:c]) for c in chunks]
    ids, combine = (jnp.transpose(v[:, 0], (0, 2, 1)) for v in (route_ids, combine_weights))
    outs = start_rows(me, residual, norm_gain, ids, combine)
    k = len(SIZES)
    xs, owns, weights, mark = list(outs[:k]), outs[k : 2 * k], outs[2 * k : 2 * k + 4], outs[-1]
    firsts = [(own, across(own, 1), across(own, 2)) for own in owns]
    weights = [weights[0], *(across(weights[bits], bits) for bits in (1, 2, 3))]
    next_gain = lax.ppermute(norm_gain, "section", [((i + 1) % sections, i) for i in range(sections)])
    mats = load_mats(mats, (mark,))
    state = {"mark": mark}
    sums = {}

    def way(step, c):
        return LAST[c] if step == STEPS - 1 else MODE[c]

    for c in chunks:
        if way(0, c) == "sums":
            xs[c] = onward(xs[c], 0)

    def apply_experts(step, c):
        own, rx, ry = firsts[c]
        rd = across(rx, 2) if c % 2 == 0 else across(ry, 1)
        carried = xs[c] if step and CARRY[c] else None
        outs = weighted_ffn(step, starts[c], (own, rx, ry, rd), weights, mats, state["mark"], carried)
        o_own, o_x, o_y, o_d, state["mark"] = outs[:5]
        if carried is not None:
            xs[c] = onward(outs[5], 0, hops(step, c))
        mine, other, bits = (o_y, o_x, 1) if c % 2 == 0 else (o_x, o_y, 2)
        part = across(o_d, bits)
        if way(step, c) == "sums":
            sums[c] = (onward(o_own, 0), onward(other, bits), mine, part)
        else:
            sums[c] = (o_own, across(other, bits), mine, part)

    def hops(step, c):
        before, now = way(step - 1, c), way(step, c)
        return (before != "sums") + (now == "sums")

    def pass_sum(step, c):
        own, got, mine, part = sums[c]
        both, state["mark"] = add_rows(mine, part, state["mark"])
        go = onward if way(step, c) == "sums" else across
        sums[c] = (own, got, go(both, 2 if c % 2 == 0 else 1))

    def move_on(step, c):
        mode = way(step, c)
        if step == STEPS - 1:
            if mode == "sums":
                return
            new, state["mark"] = add_total(xs[c], sums[c], state["mark"])
            sums[c] = ()
            xs[c] = onward(new, 0)
            return
        if mode == "whole":
            new, state["mark"] = add_total(xs[c], sums[c], state["mark"])
            xs[c] = onward(new, 0)
            return
        gain = norm_gain if mode == "sums" else next_gain
        xs[c], normed, state["mark"] = total_rows(xs[c], sums[c], gain, state["mark"])
        if mode == "rows":
            firsts[c] = tuple(onward(normed, bits) for bits in (0, 1, 2))
        else:
            firsts[c] = (normed, across(normed, 1), across(normed, 2))
        if not CARRY[c] and hops(step + 1, c):
            xs[c] = onward(xs[c], 0, hops(step + 1, c))

    def begin(step, c):
        if step < STEPS and way(step - 1, c) == "whole":
            own, state["mark"] = renorm(xs[c], norm_gain, state["mark"])
            firsts[c] = (own, across(own, 1), across(own, 2))

    for what, step, c in order(k):
        (apply_experts, pass_sum, move_on, begin)[what](step, c)
    return final_rows([(xs[c], *sums[c]) for c in chunks], residual.shape)


def per_device(residual, norm_gain, w_gate, w_up, w_down, route_ids, route_slots, combine_weights):
    mats = (w_gate[0, 0], w_up[0, 0], w_down[0, 0])
    if lax.axis_size("expert") == 4:
        return run_by_rows(residual, norm_gain, mats, route_ids, combine_weights)
    return run_by_slots(residual, norm_gain, mats, route_ids, route_slots, combine_weights)


def solution(mesh):
    in_specs = (
        P("section", "expert", None),
        P("section", None),
        P("section", "expert", None, None),
        P("section", "expert", None, None),
        P("section", "expert", None, None),
        P(None, "section", "expert", None),
        P(None, "section", "expert", None),
        P(None, "section", "expert", None),
    )
    out_specs = P("section", "expert", None)
    return jax.shard_map(
        per_device, mesh=mesh, in_specs=in_specs, out_specs=out_specs, check_vma=False
    )
```

```python
import functools

import jax
import jax.numpy as jnp
from jax import lax
from jax.experimental import pallas as pl
from jax.experimental.pallas import tpu as pltpu
from jax.sharding import PartitionSpec as P

TOP = 2
STEPS = 3
SIZES = (64, 64)
FIRST = (1, 2)
BACK = (1, 2)
MODE = ("rows", "sums")
LAST = ("rows", "sums")
LIMIT = 16 * 1024 * 1024


def order(k):
    for step in range(STEPS):
        for what in range(3):
            for c in range(k):
                yield what, step, c


def shifted(x, axis, by):
    count = lax.axis_size(axis)
    return lax.ppermute(x, axis, [(i, (i + by) % count) for i in range(count)])


def rms_normed(current, gain_row):
    inv_rms = lax.rsqrt(jnp.mean(current * current, axis=-1, keepdims=True) + 1e-06)
    return (current * inv_rms * gain_row).astype(jnp.bfloat16)


def expert_ffn(rows_in, gate_mat, up_mat, down_mat):
    gate_part = jnp.dot(rows_in, gate_mat, preferred_element_type=jnp.float32)
    upward = jnp.dot(rows_in, up_mat, preferred_element_type=jnp.float32)
    hidden = (jax.nn.silu(gate_part) * upward).astype(jnp.bfloat16)
    return jnp.dot(hidden, down_mat, preferred_element_type=jnp.float32).astype(jnp.bfloat16)


def layer_by_slots(token_rows, gain_row, chosen, slot_rows, weights_in, experts, cap, mats):
    normed = rms_normed(token_rows, gain_row)
    flat_place = chosen * cap + slot_rows
    place_iota = jnp.arange(experts * cap, dtype=jnp.int32)
    tables = [
        (flat_place[:, k : k + 1] == place_iota[None, :]).astype(jnp.bfloat16) for k in range(TOP)
    ]
    occupied = tables[0] + tables[1]
    send = lax.dot_general(
        occupied, normed, (((0,), (0,)), ((), ())), preferred_element_type=jnp.float32
    )
    send = send.astype(jnp.bfloat16).reshape(experts, cap, normed.shape[1])
    received = lax.all_to_all(send, "expert", split_axis=0, concat_axis=0, tiled=True)
    result = expert_ffn(received.reshape(experts * cap, normed.shape[1]), *mats)
    returned = lax.all_to_all(
        result.reshape(send.shape), "expert", split_axis=0, concat_axis=0, tiled=True
    ).reshape(experts * cap, normed.shape[1])
    combined = jnp.zeros(token_rows.shape, jnp.float32)
    for k in range(TOP):
        picked = jnp.dot(tables[k], returned, preferred_element_type=jnp.float32)
        combined = combined + weights_in[:, k : k + 1] * picked
    return token_rows + combined


def run_by_slots(residual, norm_gain, mats, route_ids, route_slots, combine_weights):
    experts = lax.axis_size("expert")
    cap = 4 * residual.shape[1] // experts
    current = residual[0]
    for step in range(STEPS):
        current = layer_by_slots(
            current,
            norm_gain[0],
            route_ids[step, 0],
            route_slots[step, 0],
            combine_weights[step, 0],
            experts,
            cap,
            mats,
        )
        current = shifted(current, "section", 1)
    return current[None]


def across(x, bits):
    return lax.ppermute(x, "expert", [(e, e ^ bits) for e in range(4)])


def onward(x, bits, by=1):
    sections = lax.axis_size("section")
    pairs = [
        (s * 4 + e, ((s + by) % sections) * 4 + (e ^ bits)) for s in range(sections) for e in range(4)
    ]
    return lax.ppermute(x, ("section", "expert"), pairs)


def normed_of(x, gain):
    inv_rms = lax.rsqrt(jnp.mean(x * x, axis=-1, keepdims=True) + 1e-06)
    return (x * inv_rms * gain).astype(jnp.bfloat16)


VMEM_SPEC = pl.BlockSpec(memory_space=pltpu.VMEM)
SMEM_SPEC = pl.BlockSpec(memory_space=pltpu.SMEM)
ANY_SPEC = pl.BlockSpec(memory_space=pl.ANY)
MARK = jax.ShapeDtypeStruct((8, 128), jnp.float32)


def call(kernel, outs, ins, specs, flops, moved, exps=0, scratch=(), after=()):
    ins, specs = (*after, *ins), [ANY_SPEC] * len(after) + list(specs)
    return pl.pallas_call(
        lambda *refs: kernel(*refs[len(after) :]),
        in_specs=specs,
        out_shape=outs,
        scratch_shapes=scratch,
        compiler_params=pltpu.CompilerParams(vmem_limit_bytes=LIMIT),
        cost_estimate=pl.CostEstimate(flops=flops, bytes_accessed=moved, transcendentals=exps),
    )(*ins)


def far(x):
    return pltpu.with_memory_space_constraint(x, pltpu.HBM)


def bf16_rows(n, width):
    return jax.ShapeDtypeStruct((n, width), jnp.bfloat16)


def f32_rows(n, width):
    return jax.ShapeDtypeStruct((n, width), jnp.float32)


def start_kernel(x_far, gain_far, ids_far, combine_far, *refs):
    x_refs, refs = refs[: len(SIZES)], refs[len(SIZES) :]
    normed_refs, (mark, gain, ids, combine, sems) = refs[: len(SIZES)], refs[len(SIZES) :]
    bf16, f32 = jnp.bfloat16, jnp.float32
    copies = []
    others = ((ids_far, ids), (combine_far, combine), (gain_far, gain))
    for j, (src, dst) in enumerate(others):
        copies.append(pltpu.make_async_copy(src, dst, sems.at[len(SIZES) + j]))
    at = 0
    for c, n in enumerate(SIZES):
        rows = x_far.at[0, pl.ds(at, n)]
        copies.append(pltpu.make_async_copy(rows, x_refs[c], sems.at[c]))
        at += n
    for copy in copies:
        copy.start()
    mark[...] = jnp.zeros_like(mark)
    copies[0].wait()
    copies[1].wait()
    lines = []
    for step in range(STEPS):
        for e in range(4):
            named = ids[step] == e
            lines.append(jnp.sum(jnp.where(named, combine[step], 0.0), axis=0, keepdims=True))
    tokens = ids.shape[-1]
    lines.append(jnp.zeros((32 - len(lines), tokens), f32))
    lines = jnp.concatenate(lines, axis=0)
    first = lines.astype(bf16).astype(f32)
    second = (lines - first).astype(bf16).astype(f32)
    third = lines - first - second
    blocks = [first, second, third, jnp.zeros((32, tokens), f32)]
    columns = jnp.concatenate(blocks, axis=0).T.astype(bf16)
    for copy in copies[2:]:
        copy.wait()
    at = 0
    for c, n in enumerate(SIZES):
        width = x_refs[c].shape[1]
        normed_refs[c][:, :width] = normed_of(x_refs[c][...], gain[...])
        normed_refs[c][:, width:] = columns[at : at + n]
        at += n


def start_rows(x, gain, ids, combine):
    width = x.shape[-1]
    outs = [f32_rows(n, width) for n in SIZES] + [bf16_rows(n, width + 128) for n in SIZES] + [MARK]
    scratch = [
        pltpu.VMEM(gain.shape, jnp.float32),
        pltpu.VMEM(ids.shape, jnp.int32),
        pltpu.VMEM(combine.shape, jnp.float32),
        pltpu.SemaphoreType.DMA((len(SIZES) + 3,)),
    ]
    ins = tuple(far(v) for v in (x, gain, ids, combine))
    return call(start_kernel, outs, ins, [ANY_SPEC] * 4, 5 * x.size, 6 * x.size, scratch=scratch)


def add_kernel(a_ref, b_ref, before, out_ref, mark):
    del before
    f32 = jnp.float32
    out_ref[...] = (a_ref[...].astype(f32) + b_ref[...].astype(f32)).astype(jnp.bfloat16)
    mark[...] = jnp.zeros_like(mark)


def add_rows(a, b, before, after):
    specs = [VMEM_SPEC] * 2 + [ANY_SPEC]
    outs = (bf16_rows(*a.shape), MARK)
    return call(add_kernel, outs, (a, b, before), specs, a.size, 6 * a.size, after=after)


def summed(x_ref, a_ref, b_ref):
    return x_ref[...] + (a_ref[...].astype(jnp.float32) + b_ref[...].astype(jnp.float32))


def total_kernel(x_ref, a_ref, b_ref, gain_ref, before, new_ref, normed_ref, mark):
    del before
    x = summed(x_ref, a_ref, b_ref)
    new_ref[...] = x
    normed_ref[...] = normed_of(x, gain_ref[...])
    mark[...] = jnp.zeros_like(mark)


def total_rows(sums, gain, before):
    n, width = sums[0].shape
    outs = [f32_rows(n, width), bf16_rows(n, width), MARK]
    specs = [VMEM_SPEC] * 4 + [ANY_SPEC]
    return call(total_kernel, outs, (*sums, gain, before), specs, 8 * n * width, 16 * n * width)


def last_total_kernel(x_ref, a_ref, b_ref, before, new_ref, mark):
    del before
    new_ref[...] = summed(x_ref, a_ref, b_ref)
    mark[...] = jnp.zeros_like(mark)


def last_total(sums, before):
    n, width = sums[0].shape
    specs = [VMEM_SPEC] * 3 + [ANY_SPEC]
    outs = [f32_rows(n, width), MARK]
    return call(last_total_kernel, outs, (*sums, before), specs, 3 * n * width, 12 * n * width)


def final_kernel(counts, *refs):
    out = refs[-1]
    at = i = 0
    for n, count in zip(SIZES, counts):
        out[0, at : at + n] = refs[i][...] if count == 1 else summed(*refs[i : i + 3])
        at += n
        i += count


def final_rows(groups, shape):
    out = jax.ShapeDtypeStruct(shape, jnp.float32)
    size = shape[1] * shape[2]
    ins = [v for group in groups for v in group]
    kernel = functools.partial(final_kernel, tuple(len(group) for group in groups))
    return call(kernel, out, ins, [VMEM_SPEC] * len(ins), 3 * size, 14 * size)


def experts_of(x, rows, weight, gate, up, down, waits, outs):
    f32 = jnp.float32
    waits[0]()
    gate_part = jnp.dot(rows, gate[...], preferred_element_type=f32)
    waits[1]()
    upward = jnp.dot(rows, up[...], preferred_element_type=f32)
    silu = gate_part / (1.0 + jnp.exp(-gate_part))
    hidden = (silu * upward * weight).astype(jnp.bfloat16)
    waits[2]()
    out = jnp.dot(hidden, down[...], preferred_element_type=f32)
    n = outs[0].shape[0]
    outs[0][...] = x[...] + out[:n]
    for j in range(1, 4):
        outs[j][...] = out[j * n : (j + 1) * n].astype(jnp.bfloat16)


def first_ffn_kernel(load, me_ref, x, own, rx, ry, rd, gate, up, down, *rest):
    outs, rest = rest[-6 - 4 * load :], rest[: -6 - 4 * load]
    weights, mark = outs[4], outs[5]
    waits = [lambda: None] * 3
    if load:
        mats, sems = outs[6:9], outs[9]
        copies = [
            pltpu.make_async_copy(src, dst, sems.at[j])
            for j, (src, dst) in enumerate(zip((gate, up, down), mats))
        ]
        for copy in copies:
            copy.start()
        waits = [copy.wait for copy in copies]
        gate, up, down = mats
    width = own.shape[1] - 128
    pieces = (own, rx, ry, rd)
    parts = jnp.concatenate([p[:, width:] for p in pieces], axis=0).astype(jnp.float32)
    column = lax.broadcasted_iota(jnp.int32, parts.shape, 1)
    of_steps = []
    for step in range(STEPS):
        mine = (column & 31) == 4 * step + me_ref[0]
        of_steps.append(jnp.sum(jnp.where(mine, parts, 0.0), axis=1, keepdims=True))
        weights[:, step : step + 1] = of_steps[step]
    rows = jnp.concatenate([p[:, :width] for p in pieces], axis=0)
    experts_of(x, rows, of_steps[0], gate, up, down, waits, outs[:4])
    mark[...] = jnp.zeros_like(mark)


def first_ffn(me, x, pieces, mats, load, before):
    n, width = pieces[0].shape
    width -= 128
    wide = mats[0].shape[1]
    macs = 4 * n * mats[0].size * 3
    outs = [f32_rows(n, width)] + [bf16_rows(n, width)] * 3 + [f32_rows(4 * n, 128), MARK]
    scratch = ()
    if load:
        outs += [pltpu.VMEM(m.shape, m.dtype) for m in mats]
        scratch = [pltpu.SemaphoreType.DMA((3,))]
        mats = [far(m) for m in mats]
    ins = (me, x, *pieces, *mats, *before)
    specs = [SMEM_SPEC] + [VMEM_SPEC] * 5 + [ANY_SPEC if load else VMEM_SPEC] * 3 + [ANY_SPEC] * len(before)
    kernel = functools.partial(first_ffn_kernel, load)
    return call(kernel, outs, ins, specs, 2 * macs, 16 * n * width, 4 * n * wide, scratch=scratch)


def ffn_kernel(step, x, own, rx, ry, rd, weights, gate, up, down, before, *outs):
    del before
    mine = own[...] if own.shape[0] == x.shape[0] else normed_of(x[...], own[...])
    rows = jnp.concatenate([mine, rx[...], ry[...], rd[...]], axis=0)
    experts_of(x, rows, weights[:, step : step + 1], gate, up, down, [lambda: None] * 3, outs)
    outs[4][...] = jnp.zeros_like(outs[4])


def weighted_ffn(step, x, pieces, weights, mats, before):
    n, width = x.shape
    wide = mats[0].shape[1]
    macs = 4 * n * mats[0].size * 3
    kernel = functools.partial(ffn_kernel, step)
    outs = [f32_rows(n, width)] + [bf16_rows(n, width)] * 3 + [MARK]
    ins = (x, *pieces, weights, *mats, before)
    specs = [VMEM_SPEC] * 9 + [ANY_SPEC]
    return call(kernel, outs, ins, specs, 2 * macs, 16 * n * width, 4 * n * wide)


def run_by_rows(residual, norm_gain, mats, route_ids, combine_weights):
    me = lax.axis_index("expert").reshape(1)
    k = len(SIZES)
    ids, combine = (jnp.transpose(v[:, 0], (0, 2, 1)) for v in (route_ids, combine_weights))
    outs = start_rows(residual, norm_gain, ids, combine)
    xs, owns, mark = list(outs[:k]), outs[k : 2 * k], outs[-1]
    firsts = [(own, across(own, 1), across(own, 2)) for own in owns]
    sections = lax.axis_size("section")
    next_gain = norm_gain
    if "rows" in MODE:
        next_gain = lax.ppermute(norm_gain, "section", [((i + 1) % sections, i) for i in range(sections)])
    weights = {}
    state = {"mark": mark, "mats": mats}
    sums = {}

    def way(step, c):
        return LAST[c] if step == STEPS - 1 else MODE[c]

    def apply_experts(step, c):
        own, rx, ry = firsts[c]
        rd = across(rx, 2) if FIRST[c] == 1 else across(ry, 1)
        pieces = (own, rx, ry, rd)
        if step:
            outs = weighted_ffn(step, xs[c], pieces, weights[c], state["mats"], state["mark"])
            kept, o_x, o_y, o_d, state["mark"] = outs
        else:
            outs = first_ffn(me, xs[c], pieces, state["mats"], not weights, (state["mark"], next_gain))
            kept, o_x, o_y, o_d, weights[c], state["mark"] = outs[:6]
            if len(outs) > 6:
                state["mats"] = outs[6:]
        if BACK[c] == 1:
            sums[c] = (kept, o_x, o_y, across(o_d, 1))
        else:
            sums[c] = (kept, o_y, o_x, across(o_d, 2))
        kept, other, mine, part = sums[c]
        if way(step, c) == "sums":
            sums[c] = (onward(kept, 0), onward(other, BACK[c]), mine, part)
        else:
            sums[c] = (kept, across(other, BACK[c]), mine, part)

    def pass_sum(step, c):
        kept, got, mine, part = sums[c]
        both, state["mark"] = add_rows(mine, part, state["mark"], ())
        go = onward if way(step, c) == "sums" else across
        sums[c] = (kept, got, go(both, 3 - BACK[c]))

    def move_on(step, c):
        if way(step, c) == "sums":
            if step < STEPS - 1:
                xs[c], normed, state["mark"] = total_rows(sums[c], norm_gain, state["mark"])
                firsts[c] = (normed, across(normed, 1), across(normed, 2))
            return
        if step < STEPS - 1:
            new, normed, state["mark"] = total_rows(sums[c], next_gain, state["mark"])
            firsts[c] = (norm_gain, onward(normed, 1), onward(normed, 2))
            xs[c] = onward(new, 0)
        else:
            new, state["mark"] = last_total(sums[c], state["mark"])
            sums[c] = (onward(new, 0),)

    for what, step, c in order(k):
        (apply_experts, pass_sum, move_on)[what](step, c)
    return final_rows([sums[c] for c in range(k)], residual.shape)


def per_device(residual, norm_gain, w_gate, w_up, w_down, route_ids, route_slots, combine_weights):
    mats = (w_gate[0, 0], w_up[0, 0], w_down[0, 0])
    if lax.axis_size("expert") == 4:
        return run_by_rows(residual, norm_gain, mats, route_ids, combine_weights)
    return run_by_slots(residual, norm_gain, mats, route_ids, route_slots, combine_weights)


def solution(mesh):
    in_specs = (
        P("section", "expert", None),
        P("section", None),
        P("section", "expert", None, None),
        P("section", "expert", None, None),
        P("section", "expert", None, None),
        P(None, "section", "expert", None),
        P(None, "section", "expert", None),
        P(None, "section", "expert", None),
    )
    out_specs = P("section", "expert", None)
    return jax.shard_map(
        per_device, mesh=mesh, in_specs=in_specs, out_specs=out_specs, check_vma=False
    )
```

```python
import functools

import jax
import jax.numpy as jnp
from jax import lax
from jax.experimental import pallas as pl
from jax.experimental.pallas import tpu as pltpu
from jax.sharding import PartitionSpec as P

TOP = 2
STEPS = 3
SIZES = (64, 64)
FIRST = (1, 2)
BACK = (1, 2)
MODE = ("rows", "sums")
LAST = ("sums", "sums")
LIMIT = 16 * 1024 * 1024


def order(k):
    for step in range(STEPS):
        for what in range(3):
            for c in range(k):
                yield what, step, c


def shifted(x, axis, by):
    count = lax.axis_size(axis)
    return lax.ppermute(x, axis, [(i, (i + by) % count) for i in range(count)])


def rms_normed(current, gain_row):
    inv_rms = lax.rsqrt(jnp.mean(current * current, axis=-1, keepdims=True) + 1e-06)
    return (current * inv_rms * gain_row).astype(jnp.bfloat16)


def expert_ffn(rows_in, gate_mat, up_mat, down_mat):
    gate_part = jnp.dot(rows_in, gate_mat, preferred_element_type=jnp.float32)
    upward = jnp.dot(rows_in, up_mat, preferred_element_type=jnp.float32)
    hidden = (jax.nn.silu(gate_part) * upward).astype(jnp.bfloat16)
    return jnp.dot(hidden, down_mat, preferred_element_type=jnp.float32).astype(jnp.bfloat16)


def layer_by_slots(token_rows, gain_row, chosen, slot_rows, weights_in, experts, cap, mats):
    normed = rms_normed(token_rows, gain_row)
    flat_place = chosen * cap + slot_rows
    place_iota = jnp.arange(experts * cap, dtype=jnp.int32)
    tables = [
        (flat_place[:, k : k + 1] == place_iota[None, :]).astype(jnp.bfloat16) for k in range(TOP)
    ]
    occupied = tables[0] + tables[1]
    send = lax.dot_general(
        occupied, normed, (((0,), (0,)), ((), ())), preferred_element_type=jnp.float32
    )
    send = send.astype(jnp.bfloat16).reshape(experts, cap, normed.shape[1])
    received = lax.all_to_all(send, "expert", split_axis=0, concat_axis=0, tiled=True)
    result = expert_ffn(received.reshape(experts * cap, normed.shape[1]), *mats)
    returned = lax.all_to_all(
        result.reshape(send.shape), "expert", split_axis=0, concat_axis=0, tiled=True
    ).reshape(experts * cap, normed.shape[1])
    combined = jnp.zeros(token_rows.shape, jnp.float32)
    for k in range(TOP):
        picked = jnp.dot(tables[k], returned, preferred_element_type=jnp.float32)
        combined = combined + weights_in[:, k : k + 1] * picked
    return token_rows + combined


def run_by_slots(residual, norm_gain, mats, route_ids, route_slots, combine_weights):
    experts = lax.axis_size("expert")
    cap = 4 * residual.shape[1] // experts
    current = residual[0]
    for step in range(STEPS):
        current = layer_by_slots(
            current,
            norm_gain[0],
            route_ids[step, 0],
            route_slots[step, 0],
            combine_weights[step, 0],
            experts,
            cap,
            mats,
        )
        current = shifted(current, "section", 1)
    return current[None]


def across(x, bits):
    return lax.ppermute(x, "expert", [(e, e ^ bits) for e in range(4)])


def onward(x, bits, by=1):
    sections = lax.axis_size("section")
    pairs = [
        (s * 4 + e, ((s + by) % sections) * 4 + (e ^ bits)) for s in range(sections) for e in range(4)
    ]
    return lax.ppermute(x, ("section", "expert"), pairs)


def normed_of(x, gain):
    inv_rms = lax.rsqrt(jnp.mean(x * x, axis=-1, keepdims=True) + 1e-06)
    return (x * inv_rms * gain).astype(jnp.bfloat16)


VMEM_SPEC = pl.BlockSpec(memory_space=pltpu.VMEM)
SMEM_SPEC = pl.BlockSpec(memory_space=pltpu.SMEM)
ANY_SPEC = pl.BlockSpec(memory_space=pl.ANY)
MARK = jax.ShapeDtypeStruct((8, 128), jnp.float32)


def call(kernel, outs, ins, specs, flops, moved, exps=0, scratch=(), after=()):
    ins, specs = (*after, *ins), [ANY_SPEC] * len(after) + list(specs)
    return pl.pallas_call(
        lambda *refs: kernel(*refs[len(after) :]),
        in_specs=specs,
        out_shape=outs,
        scratch_shapes=scratch,
        compiler_params=pltpu.CompilerParams(vmem_limit_bytes=LIMIT),
        cost_estimate=pl.CostEstimate(flops=flops, bytes_accessed=moved, transcendentals=exps),
    )(*ins)


def far(x):
    return pltpu.with_memory_space_constraint(x, pltpu.HBM)


def bf16_rows(n, width):
    return jax.ShapeDtypeStruct((n, width), jnp.bfloat16)


def f32_rows(n, width):
    return jax.ShapeDtypeStruct((n, width), jnp.float32)


def start_kernel(x_far, gain_far, ids_far, combine_far, *refs):
    x_refs, refs = refs[: len(SIZES)], refs[len(SIZES) :]
    normed_refs, (mark, gain, ids, combine, sems) = refs[: len(SIZES)], refs[len(SIZES) :]
    bf16, f32 = jnp.bfloat16, jnp.float32
    copies = []
    others = ((ids_far, ids), (combine_far, combine), (gain_far, gain))
    for j, (src, dst) in enumerate(others):
        copies.append(pltpu.make_async_copy(src, dst, sems.at[len(SIZES) + j]))
    at = 0
    for c, n in enumerate(SIZES):
        rows = x_far.at[0, pl.ds(at, n)]
        copies.append(pltpu.make_async_copy(rows, x_refs[c], sems.at[c]))
        at += n
    for copy in copies:
        copy.start()
    mark[...] = jnp.zeros_like(mark)
    copies[0].wait()
    copies[1].wait()
    lines = []
    for step in range(STEPS):
        for e in range(4):
            named = ids[step] == e
            lines.append(jnp.sum(jnp.where(named, combine[step], 0.0), axis=0, keepdims=True))
    tokens = ids.shape[-1]
    lines.append(jnp.zeros((32 - len(lines), tokens), f32))
    lines = jnp.concatenate(lines, axis=0)
    first = lines.astype(bf16).astype(f32)
    second = (lines - first).astype(bf16).astype(f32)
    third = lines - first - second
    blocks = [first, second, third, jnp.zeros((32, tokens), f32)]
    columns = jnp.concatenate(blocks, axis=0).T.astype(bf16)
    for copy in copies[2:]:
        copy.wait()
    at = 0
    for c, n in enumerate(SIZES):
        width = x_refs[c].shape[1]
        normed_refs[c][:, :width] = normed_of(x_refs[c][...], gain[...])
        normed_refs[c][:, width:] = columns[at : at + n]
        at += n


def start_rows(x, gain, ids, combine):
    width = x.shape[-1]
    outs = [f32_rows(n, width) for n in SIZES] + [bf16_rows(n, width + 128) for n in SIZES] + [MARK]
    scratch = [
        pltpu.VMEM(gain.shape, jnp.float32),
        pltpu.VMEM(ids.shape, jnp.int32),
        pltpu.VMEM(combine.shape, jnp.float32),
        pltpu.SemaphoreType.DMA((len(SIZES) + 3,)),
    ]
    ins = tuple(far(v) for v in (x, gain, ids, combine))
    return call(start_kernel, outs, ins, [ANY_SPEC] * 4, 5 * x.size, 6 * x.size, scratch=scratch)


def add_kernel(a_ref, b_ref, before, out_ref, mark):
    del before
    f32 = jnp.float32
    out_ref[...] = (a_ref[...].astype(f32) + b_ref[...].astype(f32)).astype(jnp.bfloat16)
    mark[...] = jnp.zeros_like(mark)


def add_rows(a, b, before, after):
    specs = [VMEM_SPEC] * 2 + [ANY_SPEC]
    outs = (bf16_rows(*a.shape), MARK)
    return call(add_kernel, outs, (a, b, before), specs, a.size, 6 * a.size, after=after)


def summed(x_ref, a_ref, b_ref):
    return x_ref[...] + (a_ref[...].astype(jnp.float32) + b_ref[...].astype(jnp.float32))


def total_kernel(x_ref, a_ref, b_ref, gain_ref, before, new_ref, normed_ref, mark):
    del before
    x = summed(x_ref, a_ref, b_ref)
    new_ref[...] = x
    normed_ref[...] = normed_of(x, gain_ref[...])
    mark[...] = jnp.zeros_like(mark)


def total_rows(sums, gain, before):
    n, width = sums[0].shape
    outs = [f32_rows(n, width), bf16_rows(n, width), MARK]
    specs = [VMEM_SPEC] * 4 + [ANY_SPEC]
    return call(total_kernel, outs, (*sums, gain, before), specs, 8 * n * width, 16 * n * width)


def last_total_kernel(x_ref, a_ref, b_ref, before, new_ref, mark):
    del before
    new_ref[...] = summed(x_ref, a_ref, b_ref)
    mark[...] = jnp.zeros_like(mark)


def last_total(sums, before):
    n, width = sums[0].shape
    specs = [VMEM_SPEC] * 3 + [ANY_SPEC]
    outs = [f32_rows(n, width), MARK]
    return call(last_total_kernel, outs, (*sums, before), specs, 3 * n * width, 12 * n * width)


def final_kernel(counts, *refs):
    out = refs[-1]
    at = i = 0
    for n, count in zip(SIZES, counts):
        out[0, at : at + n] = refs[i][...] if count == 1 else summed(*refs[i : i + 3])
        at += n
        i += count


def final_rows(groups, shape):
    out = jax.ShapeDtypeStruct(shape, jnp.float32)
    size = shape[1] * shape[2]
    ins = [v for group in groups for v in group]
    kernel = functools.partial(final_kernel, tuple(len(group) for group in groups))
    return call(kernel, out, ins, [VMEM_SPEC] * len(ins), 3 * size, 14 * size)


def experts_of(x, rows, weight, gate, up, down, waits, outs):
    f32 = jnp.float32
    waits[0]()
    gate_part = jnp.dot(rows, gate[...], preferred_element_type=f32)
    waits[1]()
    upward = jnp.dot(rows, up[...], preferred_element_type=f32)
    silu = gate_part / (1.0 + jnp.exp(-gate_part))
    hidden = (silu * upward * weight).astype(jnp.bfloat16)
    waits[2]()
    out = jnp.dot(hidden, down[...], preferred_element_type=f32)
    n = outs[0].shape[0]
    outs[0][...] = x[...] + out[:n]
    for j in range(1, 4):
        outs[j][...] = out[j * n : (j + 1) * n].astype(jnp.bfloat16)


def first_ffn_kernel(load, me_ref, x, own, rx, ry, rd, gate, up, down, *rest):
    outs, rest = rest[-6 - 4 * load :], rest[: -6 - 4 * load]
    weights, mark = outs[4], outs[5]
    waits = [lambda: None] * 3
    if load:
        mats, sems = outs[6:9], outs[9]
        copies = [
            pltpu.make_async_copy(src, dst, sems.at[j])
            for j, (src, dst) in enumerate(zip((gate, up, down), mats))
        ]
        for copy in copies:
            copy.start()
        waits = [copy.wait for copy in copies]
        gate, up, down = mats
    width = own.shape[1] - 128
    pieces = (own, rx, ry, rd)
    parts = jnp.concatenate([p[:, width:] for p in pieces], axis=0).astype(jnp.float32)
    column = lax.broadcasted_iota(jnp.int32, parts.shape, 1)
    of_steps = []
    for step in range(STEPS):
        mine = (column & 31) == 4 * step + me_ref[0]
        of_steps.append(jnp.sum(jnp.where(mine, parts, 0.0), axis=1, keepdims=True))
        weights[:, step : step + 1] = of_steps[step]
    rows = jnp.concatenate([p[:, :width] for p in pieces], axis=0)
    experts_of(x, rows, of_steps[0], gate, up, down, waits, outs[:4])
    mark[...] = jnp.zeros_like(mark)


def first_ffn(me, x, pieces, mats, load, before):
    n, width = pieces[0].shape
    width -= 128
    wide = mats[0].shape[1]
    macs = 4 * n * mats[0].size * 3
    outs = [f32_rows(n, width)] + [bf16_rows(n, width)] * 3 + [f32_rows(4 * n, 128), MARK]
    scratch = ()
    if load:
        outs += [pltpu.VMEM(m.shape, m.dtype) for m in mats]
        scratch = [pltpu.SemaphoreType.DMA((3,))]
        mats = [far(m) for m in mats]
    ins = (me, x, *pieces, *mats, *before)
    specs = [SMEM_SPEC] + [VMEM_SPEC] * 5 + [ANY_SPEC if load else VMEM_SPEC] * 3 + [ANY_SPEC] * len(before)
    kernel = functools.partial(first_ffn_kernel, load)
    return call(kernel, outs, ins, specs, 2 * macs, 16 * n * width, 4 * n * wide, scratch=scratch)


def ffn_kernel(step, x, own, rx, ry, rd, weights, gate, up, down, before, *outs):
    del before
    mine = own[...] if own.shape[0] == x.shape[0] else normed_of(x[...], own[...])
    rows = jnp.concatenate([mine, rx[...], ry[...], rd[...]], axis=0)
    experts_of(x, rows, weights[:, step : step + 1], gate, up, down, [lambda: None] * 3, outs)
    outs[4][...] = jnp.zeros_like(outs[4])


def weighted_ffn(step, x, pieces, weights, mats, before):
    n, width = x.shape
    wide = mats[0].shape[1]
    macs = 4 * n * mats[0].size * 3
    kernel = functools.partial(ffn_kernel, step)
    outs = [f32_rows(n, width)] + [bf16_rows(n, width)] * 3 + [MARK]
    ins = (x, *pieces, weights, *mats, before)
    specs = [VMEM_SPEC] * 9 + [ANY_SPEC]
    return call(kernel, outs, ins, specs, 2 * macs, 16 * n * width, 4 * n * wide)


def run_by_rows(residual, norm_gain, mats, route_ids, combine_weights):
    me = lax.axis_index("expert").reshape(1)
    k = len(SIZES)
    ids, combine = (jnp.transpose(v[:, 0], (0, 2, 1)) for v in (route_ids, combine_weights))
    outs = start_rows(residual, norm_gain, ids, combine)
    xs, owns, mark = list(outs[:k]), outs[k : 2 * k], outs[-1]
    firsts = [(own, across(own, 1), across(own, 2)) for own in owns]
    sections = lax.axis_size("section")
    next_gain = norm_gain
    if "rows" in MODE:
        next_gain = lax.ppermute(norm_gain, "section", [((i + 1) % sections, i) for i in range(sections)])
    weights = {}
    state = {"mark": mark, "mats": mats}
    sums = {}

    def way(step, c):
        return LAST[c] if step == STEPS - 1 else MODE[c]

    def apply_experts(step, c):
        own, rx, ry = firsts[c]
        rd = across(rx, 2) if FIRST[c] == 1 else across(ry, 1)
        pieces = (own, rx, ry, rd)
        if step:
            outs = weighted_ffn(step, xs[c], pieces, weights[c], state["mats"], state["mark"])
            kept, o_x, o_y, o_d, state["mark"] = outs
        else:
            outs = first_ffn(me, xs[c], pieces, state["mats"], not weights, (state["mark"], next_gain))
            kept, o_x, o_y, o_d, weights[c], state["mark"] = outs[:6]
            if len(outs) > 6:
                state["mats"] = outs[6:]
        if BACK[c] == 1:
            sums[c] = (kept, o_x, o_y, across(o_d, 1))
        else:
            sums[c] = (kept, o_y, o_x, across(o_d, 2))
        kept, other, mine, part = sums[c]
        if way(step, c) == "sums":
            sums[c] = (onward(kept, 0), onward(other, BACK[c]), mine, part)
        else:
            sums[c] = (kept, across(other, BACK[c]), mine, part)

    def pass_sum(step, c):
        kept, got, mine, part = sums[c]
        after = (kept,) if way(step, c) == "sums" and step == STEPS - 1 else ()
        both, state["mark"] = add_rows(mine, part, state["mark"], after)
        go = onward if way(step, c) == "sums" else across
        sums[c] = (kept, got, go(both, 3 - BACK[c]))

    def move_on(step, c):
        if way(step, c) == "sums":
            if step < STEPS - 1:
                xs[c], normed, state["mark"] = total_rows(sums[c], norm_gain, state["mark"])
                firsts[c] = (normed, across(normed, 1), across(normed, 2))
            return
        if step < STEPS - 1:
            new, normed, state["mark"] = total_rows(sums[c], next_gain, state["mark"])
            firsts[c] = (norm_gain, onward(normed, 1), onward(normed, 2))
            xs[c] = onward(new, 0)
        else:
            new, state["mark"] = last_total(sums[c], state["mark"])
            sums[c] = (onward(new, 0),)

    for what, step, c in order(k):
        (apply_experts, pass_sum, move_on)[what](step, c)
    return final_rows([sums[c] for c in range(k)], residual.shape)


def per_device(residual, norm_gain, w_gate, w_up, w_down, route_ids, route_slots, combine_weights):
    mats = (w_gate[0, 0], w_up[0, 0], w_down[0, 0])
    if lax.axis_size("expert") == 4:
        return run_by_rows(residual, norm_gain, mats, route_ids, combine_weights)
    return run_by_slots(residual, norm_gain, mats, route_ids, route_slots, combine_weights)


def solution(mesh):
    in_specs = (
        P("section", "expert", None),
        P("section", None),
        P("section", "expert", None, None),
        P("section", "expert", None, None),
        P("section", "expert", None, None),
        P(None, "section", "expert", None),
        P(None, "section", "expert", None),
        P(None, "section", "expert", None),
    )
    out_specs = P("section", "expert", None)
    return jax.shard_map(
        per_device, mesh=mesh, in_specs=in_specs, out_specs=out_specs, check_vma=False
    )
```

```python
import functools

import jax
import jax.numpy as jnp
from jax import lax
from jax.experimental import pallas as pl
from jax.experimental.pallas import tpu as pltpu
from jax.sharding import PartitionSpec as P

TOP = 2
STEPS = 3
SIZES = (64, 64)
FIRST = (1, 2)
BACK = (1, 2)
MODE = ("rows", "sums")
LAST = ("sums", "sums")
LIMIT = 16 * 1024 * 1024


def order(k):
    for step in range(STEPS):
        for what in range(3):
            for c in range(k):
                yield what, step, c


def shifted(x, axis, by):
    count = lax.axis_size(axis)
    return lax.ppermute(x, axis, [(i, (i + by) % count) for i in range(count)])


def rms_normed(current, gain_row):
    inv_rms = lax.rsqrt(jnp.mean(current * current, axis=-1, keepdims=True) + 1e-06)
    return (current * inv_rms * gain_row).astype(jnp.bfloat16)


def expert_ffn(rows_in, gate_mat, up_mat, down_mat):
    gate_part = jnp.dot(rows_in, gate_mat, preferred_element_type=jnp.float32)
    upward = jnp.dot(rows_in, up_mat, preferred_element_type=jnp.float32)
    hidden = (jax.nn.silu(gate_part) * upward).astype(jnp.bfloat16)
    return jnp.dot(hidden, down_mat, preferred_element_type=jnp.float32).astype(jnp.bfloat16)


def layer_by_slots(token_rows, gain_row, chosen, slot_rows, weights_in, experts, cap, mats):
    normed = rms_normed(token_rows, gain_row)
    flat_place = chosen * cap + slot_rows
    place_iota = jnp.arange(experts * cap, dtype=jnp.int32)
    tables = [
        (flat_place[:, k : k + 1] == place_iota[None, :]).astype(jnp.bfloat16) for k in range(TOP)
    ]
    occupied = tables[0] + tables[1]
    send = lax.dot_general(
        occupied, normed, (((0,), (0,)), ((), ())), preferred_element_type=jnp.float32
    )
    send = send.astype(jnp.bfloat16).reshape(experts, cap, normed.shape[1])
    received = lax.all_to_all(send, "expert", split_axis=0, concat_axis=0, tiled=True)
    result = expert_ffn(received.reshape(experts * cap, normed.shape[1]), *mats)
    returned = lax.all_to_all(
        result.reshape(send.shape), "expert", split_axis=0, concat_axis=0, tiled=True
    ).reshape(experts * cap, normed.shape[1])
    combined = jnp.zeros(token_rows.shape, jnp.float32)
    for k in range(TOP):
        picked = jnp.dot(tables[k], returned, preferred_element_type=jnp.float32)
        combined = combined + weights_in[:, k : k + 1] * picked
    return token_rows + combined


def run_by_slots(residual, norm_gain, mats, route_ids, route_slots, combine_weights):
    experts = lax.axis_size("expert")
    cap = 4 * residual.shape[1] // experts
    current = residual[0]
    for step in range(STEPS):
        current = layer_by_slots(
            current,
            norm_gain[0],
            route_ids[step, 0],
            route_slots[step, 0],
            combine_weights[step, 0],
            experts,
            cap,
            mats,
        )
        current = shifted(current, "section", 1)
    return current[None]


def across(x, bits):
    return lax.ppermute(x, "expert", [(e, e ^ bits) for e in range(4)])


def onward(x, bits, by=1):
    sections = lax.axis_size("section")
    pairs = [
        (s * 4 + e, ((s + by) % sections) * 4 + (e ^ bits)) for s in range(sections) for e in range(4)
    ]
    return lax.ppermute(x, ("section", "expert"), pairs)


def normed_of(x, gain):
    inv_rms = lax.rsqrt(jnp.mean(x * x, axis=-1, keepdims=True) + 1e-06)
    return (x * inv_rms * gain).astype(jnp.bfloat16)


VMEM_SPEC = pl.BlockSpec(memory_space=pltpu.VMEM)
SMEM_SPEC = pl.BlockSpec(memory_space=pltpu.SMEM)
ANY_SPEC = pl.BlockSpec(memory_space=pl.ANY)
MARK = jax.ShapeDtypeStruct((8, 128), jnp.float32)


def call(kernel, outs, ins, specs, flops, moved, exps=0, scratch=(), after=()):
    ins, specs = (*after, *ins), [ANY_SPEC] * len(after) + list(specs)
    return pl.pallas_call(
        lambda *refs: kernel(*refs[len(after) :]),
        in_specs=specs,
        out_shape=outs,
        scratch_shapes=scratch,
        compiler_params=pltpu.CompilerParams(vmem_limit_bytes=LIMIT),
        cost_estimate=pl.CostEstimate(flops=flops, bytes_accessed=moved, transcendentals=exps),
    )(*ins)


def far(x):
    return pltpu.with_memory_space_constraint(x, pltpu.HBM)


def bf16_rows(n, width):
    return jax.ShapeDtypeStruct((n, width), jnp.bfloat16)


def f32_rows(n, width):
    return jax.ShapeDtypeStruct((n, width), jnp.float32)


def start_kernel(x_far, gain_far, ids_far, combine_far, *refs):
    x_refs, refs = refs[: len(SIZES)], refs[len(SIZES) :]
    normed_refs, (mark, gain, ids, combine, sems) = refs[: len(SIZES)], refs[len(SIZES) :]
    bf16, f32 = jnp.bfloat16, jnp.float32
    copies = []
    others = ((ids_far, ids), (combine_far, combine), (gain_far, gain))
    for j, (src, dst) in enumerate(others):
        copies.append(pltpu.make_async_copy(src, dst, sems.at[len(SIZES) + j]))
    at = 0
    for c, n in enumerate(SIZES):
        rows = x_far.at[0, pl.ds(at, n)]
        copies.append(pltpu.make_async_copy(rows, x_refs[c], sems.at[c]))
        at += n
    for copy in copies:
        copy.start()
    mark[...] = jnp.zeros_like(mark)
    copies[0].wait()
    copies[1].wait()
    lines = []
    for step in range(STEPS):
        for e in range(4):
            named = ids[step] == e
            lines.append(jnp.sum(jnp.where(named, combine[step], 0.0), axis=0, keepdims=True))
    tokens = ids.shape[-1]
    lines.append(jnp.zeros((32 - len(lines), tokens), f32))
    lines = jnp.concatenate(lines, axis=0)
    first = lines.astype(bf16).astype(f32)
    second = (lines - first).astype(bf16).astype(f32)
    third = lines - first - second
    blocks = [first, second, third, jnp.zeros((32, tokens), f32)]
    columns = jnp.concatenate(blocks, axis=0).T.astype(bf16)
    for copy in copies[2:]:
        copy.wait()
    at = 0
    for c, n in enumerate(SIZES):
        width = x_refs[c].shape[1]
        normed_refs[c][:, :width] = normed_of(x_refs[c][...], gain[...])
        normed_refs[c][:, width:] = columns[at : at + n]
        at += n


def start_rows(x, gain, ids, combine):
    width = x.shape[-1]
    outs = [f32_rows(n, width) for n in SIZES] + [bf16_rows(n, width + 128) for n in SIZES] + [MARK]
    scratch = [
        pltpu.VMEM(gain.shape, jnp.float32),
        pltpu.VMEM(ids.shape, jnp.int32),
        pltpu.VMEM(combine.shape, jnp.float32),
        pltpu.SemaphoreType.DMA((len(SIZES) + 3,)),
    ]
    ins = tuple(far(v) for v in (x, gain, ids, combine))
    return call(start_kernel, outs, ins, [ANY_SPEC] * 4, 5 * x.size, 6 * x.size, scratch=scratch)


def add_kernel(a_ref, b_ref, before, out_ref, mark):
    del before
    f32 = jnp.float32
    out_ref[...] = (a_ref[...].astype(f32) + b_ref[...].astype(f32)).astype(jnp.bfloat16)
    mark[...] = jnp.zeros_like(mark)


def add_rows(a, b, before, after):
    specs = [VMEM_SPEC] * 2 + [ANY_SPEC]
    outs = (bf16_rows(*a.shape), MARK)
    return call(add_kernel, outs, (a, b, before), specs, a.size, 6 * a.size, after=after)


def summed(x_ref, a_ref, b_ref):
    return x_ref[...] + (a_ref[...].astype(jnp.float32) + b_ref[...].astype(jnp.float32))


def total_kernel(x_ref, a_ref, b_ref, gain_ref, before, new_ref, normed_ref, mark):
    del before
    x = summed(x_ref, a_ref, b_ref)
    new_ref[...] = x
    normed_ref[...] = normed_of(x, gain_ref[...])
    mark[...] = jnp.zeros_like(mark)


def total_rows(sums, gain, before):
    n, width = sums[0].shape
    outs = [f32_rows(n, width), bf16_rows(n, width), MARK]
    specs = [VMEM_SPEC] * 4 + [ANY_SPEC]
    return call(total_kernel, outs, (*sums, gain, before), specs, 8 * n * width, 16 * n * width)


def last_total_kernel(x_ref, a_ref, b_ref, before, new_ref, mark):
    del before
    new_ref[...] = summed(x_ref, a_ref, b_ref)
    mark[...] = jnp.zeros_like(mark)


def last_total(sums, before):
    n, width = sums[0].shape
    specs = [VMEM_SPEC] * 3 + [ANY_SPEC]
    outs = [f32_rows(n, width), MARK]
    return call(last_total_kernel, outs, (*sums, before), specs, 3 * n * width, 12 * n * width)


def final_kernel(counts, *refs):
    out = refs[-1]
    at = i = 0
    for n, count in zip(SIZES, counts):
        out[0, at : at + n] = refs[i][...] if count == 1 else summed(*refs[i : i + 3])
        at += n
        i += count


def final_rows(groups, shape):
    out = jax.ShapeDtypeStruct(shape, jnp.float32)
    size = shape[1] * shape[2]
    ins = [v for group in groups for v in group]
    kernel = functools.partial(final_kernel, tuple(len(group) for group in groups))
    return call(kernel, out, ins, [VMEM_SPEC] * len(ins), 3 * size, 14 * size)


def experts_of(x, rows, weight, gate, up, down, waits, outs):
    f32 = jnp.float32
    waits[0]()
    gate_part = jnp.dot(rows, gate[...], preferred_element_type=f32)
    waits[1]()
    upward = jnp.dot(rows, up[...], preferred_element_type=f32)
    silu = gate_part / (1.0 + jnp.exp(-gate_part))
    hidden = (silu * upward * weight).astype(jnp.bfloat16)
    waits[2]()
    out = jnp.dot(hidden, down[...], preferred_element_type=f32)
    n = outs[0].shape[0]
    outs[0][...] = x[...] + out[:n]
    for j in range(1, 4):
        outs[j][...] = out[j * n : (j + 1) * n].astype(jnp.bfloat16)


def first_ffn_kernel(load, me_ref, x, own, rx, ry, rd, gate, up, down, *rest):
    outs, rest = rest[-6 - 4 * load :], rest[: -6 - 4 * load]
    weights, mark = outs[4], outs[5]
    waits = [lambda: None] * 3
    if load:
        mats, sems = outs[6:9], outs[9]
        copies = [
            pltpu.make_async_copy(src, dst, sems.at[j])
            for j, (src, dst) in enumerate(zip((gate, up, down), mats))
        ]
        for copy in copies:
            copy.start()
        waits = [copy.wait for copy in copies]
        gate, up, down = mats
    width = own.shape[1] - 128
    pieces = (own, rx, ry, rd)
    parts = jnp.concatenate([p[:, width:] for p in pieces], axis=0).astype(jnp.float32)
    column = lax.broadcasted_iota(jnp.int32, parts.shape, 1)
    of_steps = []
    for step in range(STEPS):
        mine = (column & 31) == 4 * step + me_ref[0]
        of_steps.append(jnp.sum(jnp.where(mine, parts, 0.0), axis=1, keepdims=True))
        weights[:, step : step + 1] = of_steps[step]
    rows = jnp.concatenate([p[:, :width] for p in pieces], axis=0)
    experts_of(x, rows, of_steps[0], gate, up, down, waits, outs[:4])
    mark[...] = jnp.zeros_like(mark)


def first_ffn(me, x, pieces, mats, load, before):
    n, width = pieces[0].shape
    width -= 128
    wide = mats[0].shape[1]
    macs = 4 * n * mats[0].size * 3
    outs = [f32_rows(n, width)] + [bf16_rows(n, width)] * 3 + [f32_rows(4 * n, 128), MARK]
    scratch = ()
    if load:
        outs += [pltpu.VMEM(m.shape, m.dtype) for m in mats]
        scratch = [pltpu.SemaphoreType.DMA((3,))]
        mats = [far(m) for m in mats]
    ins = (me, x, *pieces, *mats, *before)
    specs = [SMEM_SPEC] + [VMEM_SPEC] * 5 + [ANY_SPEC if load else VMEM_SPEC] * 3 + [ANY_SPEC] * len(before)
    kernel = functools.partial(first_ffn_kernel, load)
    return call(kernel, outs, ins, specs, 2 * macs, 16 * n * width, 4 * n * wide, scratch=scratch)


def ffn_kernel(step, x, own, rx, ry, rd, weights, gate, up, down, before, *outs):
    del before
    mine = own[...] if own.shape[0] == x.shape[0] else normed_of(x[...], own[...])
    rows = jnp.concatenate([mine, rx[...], ry[...], rd[...]], axis=0)
    experts_of(x, rows, weights[:, step : step + 1], gate, up, down, [lambda: None] * 3, outs)
    outs[4][...] = jnp.zeros_like(outs[4])


def weighted_ffn(step, x, pieces, weights, mats, before):
    n, width = x.shape
    wide = mats[0].shape[1]
    macs = 4 * n * mats[0].size * 3
    kernel = functools.partial(ffn_kernel, step)
    outs = [f32_rows(n, width)] + [bf16_rows(n, width)] * 3 + [MARK]
    ins = (x, *pieces, weights, *mats, before)
    specs = [VMEM_SPEC] * 9 + [ANY_SPEC]
    return call(kernel, outs, ins, specs, 2 * macs, 16 * n * width, 4 * n * wide)


def run_by_rows(residual, norm_gain, mats, route_ids, combine_weights):
    me = lax.axis_index("expert").reshape(1)
    k = len(SIZES)
    ids, combine = (jnp.transpose(v[:, 0], (0, 2, 1)) for v in (route_ids, combine_weights))
    outs = start_rows(residual, norm_gain, ids, combine)
    xs, owns, mark = list(outs[:k]), outs[k : 2 * k], outs[-1]
    firsts = [(own, across(own, 1), across(own, 2)) for own in owns]
    sections = lax.axis_size("section")
    next_gain = norm_gain
    if "rows" in MODE:
        next_gain = lax.ppermute(norm_gain, "section", [((i + 1) % sections, i) for i in range(sections)])
    weights = {}
    state = {"mark": mark, "mats": mats}
    sums = {}

    def way(step, c):
        return LAST[c] if step == STEPS - 1 else MODE[c]

    def apply_experts(step, c):
        own, rx, ry = firsts[c]
        rd = across(rx, 2) if FIRST[c] == 1 else across(ry, 1)
        pieces = (own, rx, ry, rd)
        if step:
            outs = weighted_ffn(step, xs[c], pieces, weights[c], state["mats"], state["mark"])
            kept, o_x, o_y, o_d, state["mark"] = outs
        else:
            outs = first_ffn(me, xs[c], pieces, state["mats"], not weights, (state["mark"], next_gain))
            kept, o_x, o_y, o_d, weights[c], state["mark"] = outs[:6]
            if len(outs) > 6:
                state["mats"] = outs[6:]
        if BACK[c] == 1:
            sums[c] = (kept, o_x, o_y, across(o_d, 1))
        else:
            sums[c] = (kept, o_y, o_x, across(o_d, 2))
        kept, other, mine, part = sums[c]
        if way(step, c) == "sums":
            sums[c] = (onward(kept, 0), onward(other, BACK[c]), mine, part)
        else:
            sums[c] = (kept, across(other, BACK[c]), mine, part)

    def pass_sum(step, c):
        kept, got, mine, part = sums[c]
        after = (kept,) if way(step, c) == "sums" and step == STEPS - 1 and c == 0 else ()
        both, state["mark"] = add_rows(mine, part, state["mark"], after)
        go = onward if way(step, c) == "sums" else across
        sums[c] = (kept, got, go(both, 3 - BACK[c]))

    def move_on(step, c):
        if way(step, c) == "sums":
            if step < STEPS - 1:
                xs[c], normed, state["mark"] = total_rows(sums[c], norm_gain, state["mark"])
                firsts[c] = (normed, across(normed, 1), across(normed, 2))
            return
        if step < STEPS - 1:
            new, normed, state["mark"] = total_rows(sums[c], next_gain, state["mark"])
            firsts[c] = (norm_gain, onward(normed, 1), onward(normed, 2))
            xs[c] = onward(new, 0)
        else:
            new, state["mark"] = last_total(sums[c], state["mark"])
            sums[c] = (onward(new, 0),)

    for what, step, c in order(k):
        (apply_experts, pass_sum, move_on)[what](step, c)
    return final_rows([sums[c] for c in range(k)], residual.shape)


def per_device(residual, norm_gain, w_gate, w_up, w_down, route_ids, route_slots, combine_weights):
    mats = (w_gate[0, 0], w_up[0, 0], w_down[0, 0])
    if lax.axis_size("expert") == 4:
        return run_by_rows(residual, norm_gain, mats, route_ids, combine_weights)
    return run_by_slots(residual, norm_gain, mats, route_ids, route_slots, combine_weights)


def solution(mesh):
    in_specs = (
        P("section", "expert", None),
        P("section", None),
        P("section", "expert", None, None),
        P("section", "expert", None, None),
        P("section", "expert", None, None),
        P(None, "section", "expert", None),
        P(None, "section", "expert", None),
        P(None, "section", "expert", None),
    )
    out_specs = P("section", "expert", None)
    return jax.shard_map(
        per_device, mesh=mesh, in_specs=in_specs, out_specs=out_specs, check_vma=False
    )
```
